128 devices in a mesh: axial: 16 (over x_lo, y, core), span: 8 (over x_hi, z).
Axes of the slice: x: 4 (x_hi: 2, x_lo: 2; x = x_hi * 2 + x_lo), y: 4, z: 4, core: 2. Of those that a mesh axis runs over, the one named last changes fastest.
Arguments:
- conserved: float32 [5, 64, 32, 16384], P(None, 'span', None, 'axial'), may hold values from -6 to 6
- metric: float32 [3, 64, 32, 16384], P(None, 'span', None, 'axial'), may hold values from 0.5 to 2
- jacobian: float32 [3, 5, 5], replicated, may hold values from -2.5 to 2.5
- upper_panel: bfloat16 [32, 5, 64, 16384], P(None, None, 'span', 'axial'), may hold values from -2 to 2
- lower_panel: bfloat16 [32, 5, 64, 16384], P(None, None, 'span', 'axial'), may hold values from -2 to 2
- lower_partner: int32 [16384], P('axial'), may hold values from 0 to 16383, as said below
- upper_partner: int32 [16384], P('axial'), may hold values from 0 to 16383, as said below
- lag_phase: float32 [16384], P('axial'), may hold values from -3.140625 to 3.140625
Outputs:
- advanced: float32 [5, 64, 32, 16384], P(None, 'span', None, 'axial')
The draws below stay inside these ranges and needn't reach their ends.
Inputs may be any that keep to these rules, and one draw needn't show every extreme that they name: lower_partner[a] differs from a by at most 1024 rows, and that difference is reached. upper_partner[a] differs from a by at most 1024 rows, and that difference is reached.
All inputs are finite; a program needn't handle non-finite values.
Results may differ from the reference program's by a relative error of at most 0.0003.
Values may be sent and summed in bfloat16 or wider, within the bound.
A program may use at most 192 MiB of HBM per device.

```python
import math
import jax
import jax.numpy as jnp
from jax import lax

CA = 1024
NP = 32
HARM = 16
NA = 16384
NS = 64


def partner_table(key):
    rows = jnp.arange(NA, dtype=jnp.int32)
    offset = jax.random.randint(key, (NA,), -CA, CA + 1).astype(jnp.int32)
    middle = NA // 2
    offset = jnp.where(rows == middle - 1, CA, offset)
    offset = jnp.where(rows == middle, -CA, offset)
    return jnp.clip(rows + offset, 0, NA - 1).astype(jnp.int32)


def draw_lower_partner(key, part):
    key = jax.random.fold_in(key, 11)
    return partner_table(key)


def draw_upper_partner(key, part):
    key = jax.random.fold_in(key, 12)
    return partner_table(key)


def block_levels(key, dims, split, low, top_value):
    def one(position, blocks):
        draws = jax.random.uniform(jax.random.fold_in(jax.random.fold_in(key, 6), position), (blocks,), jnp.float32, low / len(split), top_value / len(split))
        return jnp.repeat(jnp.exp(draws), dims[position] // blocks).reshape((-1,) + (1,) * (len(dims) - position - 1))

    level = one(*split[0])
    for cut in split[1:]:
        level = level * one(*cut)
    return level


def normal_values(own_key, shape, width, reach, shards=(), kind=jnp.bfloat16):
    drawn = width * jax.random.normal(own_key, shape, jnp.float32)
    if shards:
        drawn = drawn * block_levels(own_key, shape, shards, -0.22, 0.18)
    return jnp.clip(drawn, -reach, reach).astype(kind)


def setup_inputs(seed: int = 0) -> dict:
    splits = jax.random.split(jax.random.key(seed), 9)
    return {
        "conserved": normal_values(splits[0], (5, NS, NP, NA), 1.0, 6.0, ((1, 8), (3, 16)), jnp.float32),
        "metric": jnp.clip(jnp.exp(math.log(2.0) - 1.3862944 * jax.random.uniform(splits[1], (3, NS, NP, NA), jnp.float32) ** block_levels(splits[1], (3, NS, NP, NA), ((1, 8), (3, 16)), -0.2, 0.2)), 0.5, 2.0),
        "jacobian": normal_values(splits[2], (3, 5, 5), 5 ** -0.5, 2.5, (), jnp.float32),
        "upper_panel": normal_values(splits[3], (2 * HARM, 5, NS, NA), 0.3, 2.0, ((2, 8), (3, 16))),
        "lower_panel": normal_values(splits[4], (2 * HARM, 5, NS, NA), 0.3, 2.0, ((2, 8), (3, 16))),
        "lower_partner": draw_lower_partner(jax.random.fold_in(splits[8], 71), 0),
        "upper_partner": draw_upper_partner(jax.random.fold_in(splits[8], 71), 0),
        "lag_phase": jnp.clip(jax.random.uniform(splits[7], (NA,), jnp.float32, -3.140625, 3.140625), -3.140625, 3.140625),
    }


viscosity = 0.05
step_size = 0.2


def basis(phase):
    orders = jnp.arange(HARM).astype(jnp.float32)
    angles = orders[:, None] * phase[None, :]
    return jnp.stack([jnp.cos(angles), jnp.sin(angles)], axis=1).reshape(2 * HARM, phase.shape[0])


def reference(conserved, metric, jacobian, upper_panel, lower_panel, lower_partner, upper_partner, lag_phase):
    lower_basis = basis(lag_phase)
    upper_basis = basis(-lag_phase)
    picked_upper = jnp.take(upper_panel, lower_partner, axis=3).astype(jnp.float32)
    lower_ghost = jnp.einsum('mfsa,ma->fsa', picked_upper, lower_basis, precision=lax.Precision.HIGHEST)
    picked_lower = jnp.take(lower_panel, upper_partner, axis=3).astype(jnp.float32)
    upper_ghost = jnp.einsum('mfsa,ma->fsa', picked_lower, upper_basis, precision=lax.Precision.HIGHEST)
    padded = jnp.pad(conserved, ((0, 0), (1, 1), (0, 0), (1, 1)))
    pitched = jnp.concatenate([lower_ghost[:, :, None, :], conserved, upper_ghost[:, :, None, :]], axis=2)
    pairs = [(padded[:, 1:-1, :, 2:], padded[:, 1:-1, :, :-2]),
             (padded[:, 2:, :, 1:-1], padded[:, :-2, :, 1:-1]),
             (pitched[:, :, 2:, :], pitched[:, :, :-2, :])]
    rate = jnp.zeros_like(conserved)
    for which in range(3):
        upward, downward = pairs[which]
        mixed = jnp.einsum('fg,gspa->fspa', jacobian[which], upward - downward, precision=lax.Precision.HIGHEST)
        rate = rate + metric[which][None] * (-0.5 * mixed + viscosity * (upward + downward - 2.0 * conserved))
    return conserved + step_size * rate
```

```python
import functools

import jax
import jax.numpy as jnp
from jax import lax
from jax.experimental import pallas as pl
from jax.experimental.pallas import tpu as pltpu
from jax.sharding import PartitionSpec as P

f32 = jnp.float32
bf16 = jnp.bfloat16
MESH = pl.DeviceIdType.MESH

FIELDS = 5
LAYERS = 8
PITCH = 32
ROWS = 1024
MODES = 32
FS = FIELDS * LAYERS
FP = FIELDS * PITCH
TILE = 256
TILES = ROWS // TILE
PAIRS = 2 * TILES - 1
OWN, LEFT, RIGHT = 0, 1, 2


def row_of(x):
    return jnp.concatenate([x[r : r + 1, :] for r in range(8)], axis=1)


def split2(x):
    high = x.astype(bf16)
    return high, (x - high.astype(f32)).astype(bf16)


def split3(x):
    high = x.astype(bf16).astype(f32)
    rest = x - high
    middle = rest.astype(bf16).astype(f32)
    return [high, middle, rest - middle]


def one_hot(places):
    inside = (places >= 0.0) & (places < TILE)
    wanted = jnp.where(inside, places, -1.0).astype(bf16)
    out = []
    for j in range(places.shape[1] // TILE):
        k = lax.broadcasted_iota(jnp.int32, (TILE, TILE), 0).astype(bf16)
        w = wanted[:, j * TILE : (j + 1) * TILE]
        out.append(jnp.where(k == w, bf16(1), bf16(0)))
    return out


def sort_rows(partner, cosine, sine, order):
    index = lax.broadcasted_iota(jnp.int32, (8, 128), 0) * 128 + lax.broadcasted_iota(
        jnp.int32, (8, 128), 1
    )
    key = (partner * ROWS + index).astype(f32)
    counts = [jnp.zeros((8, 128), f32) for _ in range(8)]
    for c in range(8):
        column = jnp.transpose(jnp.broadcast_to(key[c : c + 1, :], (128, 128)))
        for r in range(8):
            less = jnp.where(column < key[r : r + 1, :], 1.0, 0.0)
            counts[r] = counts[r] + jnp.sum(less.reshape(16, 8, 128), axis=0)
    rank = jnp.concatenate([jnp.sum(c, axis=0, keepdims=True) for c in counts], axis=1)
    for t in range(TILES):
        for j, block in enumerate(one_hot(rank - float(t * TILE))):
            order[t * TILE : (t + 1) * TILE, j * TILE : (j + 1) * TILE] = block
    pieces = [(partner // 256).astype(f32), (partner % 256).astype(f32)]
    pieces += split3(cosine) + split3(sine)
    values = jnp.concatenate([row_of(x) for x in pieces] + [jnp.zeros((8, ROWS), f32)], axis=0)
    placed = lax.dot_general(
        values.astype(bf16), order[...], (((1,), (1,)), ((), ())), preferred_element_type=f32
    )
    return (
        placed[0:1] * 256.0 + placed[1:2],
        (placed[4:5] + placed[3:4]) + placed[2:3],
        (placed[7:8] + placed[6:7]) + placed[5:6],
    )


def fill_basis(cosine, sine, basis):
    c, s = jnp.ones_like(cosine), jnp.zeros_like(sine)
    n = cosine.shape[0]
    for k in range(MODES // 2):
        for j in range(TILES):
            basis[j, 2 * k, 0:n, :] = c[:, j * TILE : (j + 1) * TILE]
            basis[j, 2 * k + 1, 0:n, :] = s[:, j * TILE : (j + 1) * TILE]
        c, s = c * cosine - s * sine, s * cosine + c * sine


def evaluate(panel, basis, line, sorted_row, raw, first_row, parts, ghost):
    bounds = [jnp.sum((raw < first_row + t * TILE).astype(jnp.int32)) for t in range(TILES + 1)]
    start = first_row.astype(f32)
    tile = jnp.int32(0)
    block = jnp.minimum(bounds[0] // TILE, TILES - 1)
    blocks = []
    for i in range(PAIRS):
        used = jnp.minimum(tile, TILES - 1)
        row = sorted_row[:, 0:TILE]
        for j in range(1, TILES):
            row = jnp.where(block == j, sorted_row[:, j * TILE : (j + 1) * TILE], row)
        shift = jnp.where(tile < TILES, (tile * TILE).astype(f32), 1.0e6)
        chosen = one_hot(row - (start + shift))[0]
        total = None
        half = MODES // 2
        for h in range(2):
            picked = jnp.dot(
                panel[used, h * half * FS : (h + 1) * half * FS, :],
                chosen,
                preferred_element_type=f32,
            )
            for m in range(half):
                weight = basis[block, h * half + m, line : line + 1, :]
                term = picked[m * FS : (m + 1) * FS] * weight
                total = term if total is None else total + term
        parts[i] = total
        blocks.append(block)
        end = bounds[TILES]
        for t in range(TILES - 1, 0, -1):
            end = jnp.where(tile == t - 1, bounds[t], end)
        over = (end > (block + 1) * TILE) & (block < TILES - 1) & (tile < TILES)
        tile = jnp.where(over, tile, tile + 1)
        block = jnp.where(over, block + 1, block)
    for j in range(TILES):
        total = jnp.zeros((FS, TILE), f32)
        for i in range(PAIRS):
            total = total + parts[i] * (blocks[i] == j).astype(f32)
        ghost[:, j * TILE : (j + 1) * TILE] = total


def fill_stencil(jacobian, stencil):
    column = lax.broadcasted_iota(jnp.int32, (PITCH, 512), 1)
    row = lax.broadcasted_iota(jnp.int32, (PITCH, 512), 0)
    third = jnp.where(column < FP, 0, jnp.where(column < 2 * FP, 1, jnp.where(column < 3 * FP, 2, 3)))
    place = column - FP * third
    field = jnp.where(third < 3, place // PITCH, -1)
    cell = place % PITCH
    here = cell == row
    above = cell == row + 1
    below = cell == row - 1
    for block, d in enumerate((2, 1, 0)):
        for f in range(FIELDS):
            weight = jnp.zeros((PITCH, 512), f32)
            for g in range(FIELDS):
                weight = jnp.where(field == g, -0.1 * jacobian[f, d, g], weight)
            smooth = jnp.where(field == f, f32(0.01), f32(0.0))
            if d == 2:
                value = jnp.where(above, smooth + weight, jnp.where(below, smooth - weight, 0.0))
            else:
                value = jnp.where(here, smooth + weight, 0.0)
            high = value.astype(bf16).astype(f32)
            value = jnp.where(third == 2, value - high, high)
            at = (block * FIELDS + f) * PITCH
            stencil[at : at + PITCH, :] = value.astype(bf16)


def stacked(x):
    high, low = split2(x)
    return jnp.concatenate([high, low, high, jnp.zeros((32, x.shape[1]), bf16)], axis=0)


def slot(s):
    return 0 if s == 0 else 1 if s == LAYERS - 1 else 2 + s % 3


def kernel(
    lower_partner,
    upper_partner,
    phase_ref,
    jacobian,
    u_hbm,
    metric_hbm,
    upper_hbm,
    lower_hbm,
    out,
    u,
    metric,
    panel,
    order,
    sorted_own,
    sorted_in,
    partner_ref,
    raw_in,
    basis_own,
    basis_in,
    parts,
    ghost_own,
    ghost_out,
    ghost_in,
    halo,
    edge_out,
    edge_in,
    edge_add,
    fix,
    stencil,
    pitch_part,
    span_part,
    axial_part,
    u_sem,
    metric_sem,
    panel_sem,
    send_sem,
    recv_sem,
):
    axial, span = lax.axis_index("axial"), lax.axis_index("span")
    axial_last, span_last = lax.axis_size("axial") - 1, lax.axis_size("span") - 1
    has_left, has_right = axial > 0, axial < axial_last
    has_down, has_up = span > 0, span < span_last
    left = {"axial": jnp.maximum(axial - 1, 0)}
    right = {"axial": jnp.minimum(axial + 1, axial_last)}
    down = {"span": jnp.maximum(span - 1, 0)}
    up = {"span": jnp.minimum(span + 1, span_last)}
    sides = ((has_left, left), (has_right, right))

    u_copies = [pltpu.make_async_copy(u_hbm.at[:, s], u.at[:, s], u_sem.at[s]) for s in range(LAYERS)]
    metric_copies = [
        pltpu.make_async_copy(metric_hbm.at[:, s], metric.at[:, s], metric_sem.at[s])
        for s in range(LAYERS)
    ]
    panel_copies = [
        pltpu.make_async_copy(
            hbm.at[:, t * TILE : (t + 1) * TILE], panel.at[i, t], panel_sem.at[i, t]
        )
        for i, hbm in enumerate((upper_hbm, lower_hbm))
        for t in range(TILES)
    ]
    for c in panel_copies + u_copies + metric_copies:
        c.start()

    for i, (present, _) in enumerate(sides):

        @pl.when(jnp.logical_not(present))
        def _():
            sorted_in[i] = jnp.zeros((8, ROWS), f32)
            raw_in[i] = jnp.zeros((2, 8, 128), jnp.int32)
            ghost_in[i] = jnp.zeros((2, FS, ROWS), f32)
            edge_in[i] = jnp.zeros((FIELDS, PITCH, 128), f32)

    for i, present in enumerate((has_down, has_up)):

        @pl.when(jnp.logical_not(present))
        def _():
            halo[i] = jnp.zeros((FIELDS, PITCH, ROWS), f32)

    barrier = pltpu.get_barrier_semaphore()
    around = sides + ((has_down, down), (has_up, up))
    for present, device in around:

        @pl.when(present)
        def _():
            pl.semaphore_signal(barrier, inc=1, device_id=device, device_id_type=MESH)

    partner_ref[0] = lower_partner[...]
    partner_ref[1] = upper_partner[...]
    fill_stencil(jacobian, stencil)
    cosine, sine = jnp.cos(phase_ref[...]), jnp.sin(phase_ref[...])
    upper_sorted = sort_rows(partner_ref[0], cosine, sine, order.at[0])
    lower_sorted = sort_rows(partner_ref[1], cosine, -sine, order.at[1])
    lines = [x for pair in zip(upper_sorted, lower_sorted) for x in pair]
    sorted_own[...] = jnp.concatenate(lines + [jnp.zeros((2, ROWS), f32)], axis=0)

    pl.semaphore_wait(barrier, sum(present.astype(jnp.int32) for present, _ in around))

    def remote(number, source, target, device):
        return pltpu.make_async_remote_copy(
            src_ref=source,
            dst_ref=target,
            send_sem=send_sem.at[number],
            recv_sem=recv_sem.at[number],
            device_id=device,
            device_id_type=MESH,
        )

    def tables(i, device):
        return [
            remote(i, sorted_own, sorted_in.at[1 - i], device),
            remote(2 + i, partner_ref, raw_in.at[1 - i], device),
        ]

    def edges(i, device):
        return remote(4 + i, edge_out.at[i], edge_in.at[1 - i], device)

    def ghosts(i, device):
        return remote(6 + i, ghost_out.at[i], ghost_in.at[1 - i], device)

    def halos(i, device):
        layer = 0 if i == 0 else LAYERS - 1
        return remote(8 + i, u_hbm.at[:, layer], halo.at[1 - i], device)

    for i, (present, device) in enumerate(sides):

        @pl.when(present)
        def _():
            for c in tables(i, device):
                c.start()

    for i, (present, device) in enumerate(((has_down, down), (has_up, up))):

        @pl.when(present)
        def _():
            halos(i, device).start()

    fill_basis(sorted_own[2:4], sorted_own[4:6], basis_own)

    first_row = axial * ROWS

    for c in panel_copies:
        c.wait()

    for i in range(2):
        evaluate(
            panel.at[i], basis_own, i, sorted_own[i : i + 1], partner_ref[i], first_row, parts,
            ghost_own.at[i],
        )

    for c in u_copies:
        c.wait()
    lane = lax.broadcasted_iota(jnp.int32, (PITCH, 128), 1)
    for i, (at, turn) in enumerate(((0, 0), (ROWS - 128, 1))):
        for f in range(FIELDS):
            packed = jnp.zeros((PITCH, 128), f32)
            for s in range(LAYERS):
                turned = u[f, s, :, at : at + 128]
                if (s + turn) % 128:
                    turned = pltpu.roll(turned, s + turn, 1)
                packed = jnp.where(lane == s, turned, packed)
            edge_out[i, f] = packed
    for i, (present, device) in enumerate(sides):

        @pl.when(present)
        def _():
            edges(i, device).start()

    for i, (present, device) in enumerate(sides):

        @pl.when(present)
        def _():
            for c in tables(1 - i, device):
                c.wait_recv()

    fill_basis(
        jnp.concatenate([sorted_in[0, 2:4], sorted_in[1, 2:4]], axis=0),
        jnp.concatenate([sorted_in[0, 4:6], sorted_in[1, 4:6]], axis=0),
        basis_in,
    )
    for i, (present, device) in enumerate(sides):
        for p in range(2):
            evaluate(
                panel.at[p], basis_in, 2 * i + p, sorted_in[i, p : p + 1], raw_in[i, p], first_row,
                parts, ghost_out.at[i, p],
            )

        @pl.when(present)
        def _():
            ghosts(i, device).start()

    def products(s):
        for t in range(TILES):
            at = slice(t * TILE, (t + 1) * TILE)
            x = stacked(u[:, s, :, at].reshape(FP, TILE))
            y = jnp.dot(stencil[...], x, preferred_element_type=f32)
            pitch_part[slot(s), :, at] = y[0:FP]
            span_part[s + 1, :, at] = y[FP : 2 * FP]
            axial_part[slot(s), :, at] = y[2 * FP : 3 * FP]

    def outside(i):
        for t in range(TILES):
            at = slice(t * TILE, (t + 1) * TILE)
            x = stacked(halo[i, :, :, at].reshape(FP, TILE))
            y = jnp.dot(stencil[FP : 2 * FP, :], x, preferred_element_type=f32)
            span_part[i * (LAYERS + 1), :, at] = y

    lane8 = lax.broadcasted_iota(jnp.int32, (8, 128), 1)

    def combine(s):
        for t in range(PITCH // 8):
            r = slice(8 * t, 8 * t + 8)
            m = [metric[d, s, r, :] for d in range(3)]
            keep = 1.0 - 0.02 * (m[0] + m[1] + m[2])
            for f in range(FIELDS):
                rr = slice(PITCH * f + 8 * t, PITCH * f + 8 * t + 8)
                here = u[f, s, r, :]
                y = axial_part[slot(s), rr, :]
                after = pltpu.roll(y, ROWS - 1, 1)
                before = pltpu.roll(y - 0.02 * here, 1, 1)
                after_in = pltpu.roll(edge_add[1, f, r, :], (127 - s) % 128, 1)
                before_in = edge_add[0, f, r, :]
                if s:
                    before_in = pltpu.roll(before_in, 128 - s, 1)
                along = jnp.concatenate(
                    [
                        after[:, :128] - jnp.where(lane8 == 0, before_in, before[:, :128]),
                        after[:, 128:-128] - before[:, 128:-128],
                        jnp.where(lane8 == 127, after_in, after[:, -128:]) - before[:, -128:],
                    ],
                    axis=1,
                )
                lower = u[f, s - 1, r, :] if s else halo[0, f, r, :]
                across = span_part[s + 2, rr, :] - span_part[s, rr, :] + 0.02 * lower
                out[f, s, r, :] = (
                    keep * here + m[2] * pitch_part[slot(s), rr, :] + m[1] * across + m[0] * along
                )

    def patch(s):
        for f in range(FIELDS):
            for i, p in enumerate((0, PITCH - 1)):
                out[f, s, p : p + 1, :] = out[f, s, p : p + 1, :] + fix[i, f, s : s + 1, :]

    for c in metric_copies:
        c.wait()
    products(0)
    products(1)

    for i, (present, device) in enumerate(sides):

        @pl.when(present)
        def _():
            edges(1 - i, device).wait_recv()

    for i, sign in ((0, -0.01), (1, 0.01)):
        for f in range(FIELDS):
            total = sign * edge_in[i, f]
            for g in range(FIELDS):
                total = total + (-0.1 * jacobian[f, 0, g]) * edge_in[i, g]
            edge_add[i, f] = total

    for s in range(2, LAYERS):
        products(s)
        combine(s - 1)

    for i, (present, device) in enumerate(sides):

        @pl.when(present)
        def _():
            ghosts(1 - i, device).wait_recv()

    for i, (p, sign) in enumerate(((0, 0.1), (PITCH - 1, -0.1))):
        total = ghost_own[i] + ghost_in[0, i] + ghost_in[1, i]
        high, low = split2(total)
        both = jnp.dot(
            jnp.concatenate([high, low], axis=0), order[i], preferred_element_type=f32
        )
        ghost = both[0:FS] + both[FS : 2 * FS]
        scale = jnp.concatenate([metric[2, s, p : p + 1, :] for s in range(LAYERS)], axis=0)
        for f in range(FIELDS):
            total = 0.01 * ghost[f * LAYERS : (f + 1) * LAYERS]
            for g in range(FIELDS):
                total = total + (sign * jacobian[f, 2, g]) * ghost[g * LAYERS : (g + 1) * LAYERS]
            fix[i, f] = scale * total
    for s in range(1, LAYERS - 1):
        patch(s)

    for i, (present, device) in enumerate(((has_down, down), (has_up, up))):

        @pl.when(present)
        def _():
            halos(1 - i, device).wait_recv()

        outside(i)
        s = 0 if i == 0 else LAYERS - 1
        combine(s)
        patch(s)

    for i, (present, device) in enumerate(sides):

        @pl.when(present)
        def _():
            for c in tables(i, device) + [edges(i, device), ghosts(i, device)]:
                c.wait_send()

    for i, (present, device) in enumerate(((has_down, down), (has_up, up))):

        @pl.when(present)
        def _():
            halos(i, device).wait_send()


def on_device(
    conserved, metric, jacobian, upper_panel, lower_panel, lower_partner, upper_partner, lag_phase
):
    rows = [x.reshape(8, 128) for x in (lower_partner, upper_partner, lag_phase)]
    jacobian = jnp.transpose(jacobian, (1, 0, 2))
    upper = upper_panel.reshape(MODES * FS, ROWS)
    lower = lower_panel.reshape(MODES * FS, ROWS)
    vmem = pl.BlockSpec(memory_space=pltpu.VMEM)
    anywhere = pl.BlockSpec(memory_space=pl.ANY)
    shape = (FIELDS, LAYERS, PITCH, ROWS)
    return pl.pallas_call(
        kernel,
        out_shape=jax.ShapeDtypeStruct(shape, f32),
        in_specs=[vmem, vmem, vmem, pl.BlockSpec(memory_space=pltpu.SMEM)] + [anywhere] * 4,
        out_specs=vmem,
        scratch_shapes=[
            pltpu.VMEM(shape, f32),
            pltpu.VMEM((3, LAYERS, PITCH, ROWS), f32),
            pltpu.VMEM((2, TILES, MODES * FS, TILE), bf16),
            pltpu.VMEM((2, ROWS, ROWS), bf16),
            pltpu.VMEM((8, ROWS), f32),
            pltpu.VMEM((2, 8, ROWS), f32),
            pltpu.VMEM((2, 8, 128), jnp.int32),
            pltpu.VMEM((2, 2, 8, 128), jnp.int32),
            pltpu.VMEM((TILES, MODES, 8, TILE), f32),
            pltpu.VMEM((TILES, MODES, 8, TILE), f32),
            pltpu.VMEM((PAIRS, FS, TILE), f32),
            pltpu.VMEM((2, FS, ROWS), f32),
            pltpu.VMEM((2, 2, FS, ROWS), f32),
            pltpu.VMEM((2, 2, FS, ROWS), f32),
            pltpu.VMEM((2, FIELDS, PITCH, ROWS), f32),
            pltpu.VMEM((2, FIELDS, PITCH, 128), f32),
            pltpu.VMEM((2, FIELDS, PITCH, 128), f32),
            pltpu.VMEM((2, FIELDS, PITCH, 128), f32),
            pltpu.VMEM((2, FIELDS, LAYERS, ROWS), f32),
            pltpu.VMEM((3 * FP, 512), bf16),
            pltpu.VMEM((5, FP, ROWS), f32),
            pltpu.VMEM((LAYERS + 2, FP, ROWS), f32),
            pltpu.VMEM((5, FP, ROWS), f32),
            pltpu.SemaphoreType.DMA((LAYERS,)),
            pltpu.SemaphoreType.DMA((LAYERS,)),
            pltpu.SemaphoreType.DMA((2, TILES)),
            pltpu.SemaphoreType.DMA((10,)),
            pltpu.SemaphoreType.DMA((10,)),
        ],
        compiler_params=pltpu.CompilerParams(
            collective_id=0, has_side_effects=True, vmem_limit_bytes=58 * 2**20
        ),
        name="section",
    )(*rows, jacobian, conserved, metric, upper, lower)


def solution(mesh):
    in_specs = (
        P(None, "span", None, "axial"),
        P(None, "span", None, "axial"),
        P(),
        P(None, None, "span", "axial"),
        P(None, None, "span", "axial"),
        P("axial"),
        P("axial"),
        P("axial"),
    )
    out_specs = P(None, "span", None, "axial")
    return jax.shard_map(
        on_device, mesh=mesh, in_specs=in_specs, out_specs=out_specs, check_vma=False
    )
```

```python
import functools

import jax
import jax.numpy as jnp
from jax import lax
from jax.experimental import pallas as pl
from jax.experimental.pallas import tpu as pltpu
from jax.sharding import PartitionSpec as P

f32 = jnp.float32
bf16 = jnp.bfloat16
MESH = pl.DeviceIdType.MESH

FIELDS = 5
LAYERS = 8
PITCH = 32
ROWS = 1024
MODES = 32
FS = FIELDS * LAYERS
FP = FIELDS * PITCH
TILE = 256
TILES = ROWS // TILE
PAIRS = 2 * TILES - 1
OWN, LEFT, RIGHT = 0, 1, 2


def row_of(x):
    return jnp.concatenate([x[r : r + 1, :] for r in range(8)], axis=1)


def split2(x):
    high = x.astype(bf16)
    return high, (x - high.astype(f32)).astype(bf16)


def split3(x):
    high = x.astype(bf16).astype(f32)
    rest = x - high
    middle = rest.astype(bf16).astype(f32)
    return [high, middle, rest - middle]


def one_hot(places):
    inside = (places >= 0.0) & (places < TILE)
    wanted = jnp.where(inside, places, -1.0).astype(bf16)
    out = []
    for j in range(places.shape[1] // TILE):
        k = lax.broadcasted_iota(jnp.int32, (TILE, TILE), 0).astype(bf16)
        w = wanted[:, j * TILE : (j + 1) * TILE]
        out.append(jnp.where(k == w, bf16(1), bf16(0)))
    return out


def sort_rows(partner, cosine, sine, order):
    index = lax.broadcasted_iota(jnp.int32, (8, 128), 0) * 128 + lax.broadcasted_iota(
        jnp.int32, (8, 128), 1
    )
    key = (partner * ROWS + index).astype(f32)
    counts = [jnp.zeros((8, 128), f32) for _ in range(8)]
    for c in range(8):
        column = jnp.transpose(jnp.broadcast_to(key[c : c + 1, :], (128, 128)))
        for r in range(8):
            less = jnp.where(column < key[r : r + 1, :], 1.0, 0.0)
            counts[r] = counts[r] + jnp.sum(less.reshape(16, 8, 128), axis=0)
    rank = jnp.concatenate([jnp.sum(c, axis=0, keepdims=True) for c in counts], axis=1)
    for t in range(TILES):
        for j, block in enumerate(one_hot(rank - float(t * TILE))):
            order[t * TILE : (t + 1) * TILE, j * TILE : (j + 1) * TILE] = block
    pieces = [(partner // 256).astype(f32), (partner % 256).astype(f32)]
    pieces += split3(cosine) + split3(sine)
    values = jnp.concatenate([row_of(x) for x in pieces] + [jnp.zeros((8, ROWS), f32)], axis=0)
    placed = lax.dot_general(
        values.astype(bf16), order[...], (((1,), (1,)), ((), ())), preferred_element_type=f32
    )
    return (
        placed[0:1] * 256.0 + placed[1:2],
        (placed[4:5] + placed[3:4]) + placed[2:3],
        (placed[7:8] + placed[6:7]) + placed[5:6],
    )


def fill_basis(cosine, sine, basis):
    c, s = jnp.ones_like(cosine), jnp.zeros_like(sine)
    n = cosine.shape[0]
    for k in range(MODES // 2):
        for j in range(TILES):
            basis[j, 2 * k, 0:n, :] = c[:, j * TILE : (j + 1) * TILE]
            basis[j, 2 * k + 1, 0:n, :] = s[:, j * TILE : (j + 1) * TILE]
        c, s = c * cosine - s * sine, s * cosine + c * sine


def evaluate(panel, basis, line, sorted_row, raw, first_row, parts, ghost):
    bounds = [jnp.sum((raw < first_row + t * TILE).astype(jnp.int32)) for t in range(TILES + 1)]
    start = first_row.astype(f32)
    tile = jnp.int32(0)
    block = jnp.minimum(bounds[0] // TILE, TILES - 1)
    blocks = []
    for i in range(PAIRS):
        used = jnp.minimum(tile, TILES - 1)
        row = sorted_row[:, 0:TILE]
        for j in range(1, TILES):
            row = jnp.where(block == j, sorted_row[:, j * TILE : (j + 1) * TILE], row)
        shift = jnp.where(tile < TILES, (tile * TILE).astype(f32), 1.0e6)
        chosen = one_hot(row - (start + shift))[0]
        total = None
        half = MODES // 2
        for h in range(2):
            picked = jnp.dot(
                panel[used, h * half * FS : (h + 1) * half * FS, :],
                chosen,
                preferred_element_type=f32,
            )
            for m in range(half):
                weight = basis[block, h * half + m, line : line + 1, :]
                term = picked[m * FS : (m + 1) * FS] * weight
                total = term if total is None else total + term
        parts[i] = total
        blocks.append(block)
        end = bounds[TILES]
        for t in range(TILES - 1, 0, -1):
            end = jnp.where(tile == t - 1, bounds[t], end)
        over = (end > (block + 1) * TILE) & (block < TILES - 1) & (tile < TILES)
        tile = jnp.where(over, tile, tile + 1)
        block = jnp.where(over, block + 1, block)
    for j in range(TILES):
        total = jnp.zeros((FS, TILE), f32)
        for i in range(PAIRS):
            total = total + parts[i] * (blocks[i] == j).astype(f32)
        ghost[:, j * TILE : (j + 1) * TILE] = total


def fill_stencil(jacobian, stencil):
    column = lax.broadcasted_iota(jnp.int32, (PITCH, 512), 1)
    row = lax.broadcasted_iota(jnp.int32, (PITCH, 512), 0)
    third = jnp.where(column < FP, 0, jnp.where(column < 2 * FP, 1, jnp.where(column < 3 * FP, 2, 3)))
    place = column - FP * third
    field = jnp.where(third < 3, place // PITCH, -1)
    cell = place % PITCH
    here = cell == row
    above = cell == row + 1
    below = cell == row - 1
    for block, d in enumerate((2, 1, 0)):
        for f in range(FIELDS):
            weight = jnp.zeros((PITCH, 512), f32)
            for g in range(FIELDS):
                weight = jnp.where(field == g, -0.1 * jacobian[f, d, g], weight)
            smooth = jnp.where(field == f, f32(0.01), f32(0.0))
            if d == 2:
                value = jnp.where(above, smooth + weight, jnp.where(below, smooth - weight, 0.0))
            else:
                value = jnp.where(here, smooth + weight, 0.0)
            high = value.astype(bf16).astype(f32)
            value = jnp.where(third == 2, value - high, high)
            at = (block * FIELDS + f) * PITCH
            stencil[at : at + PITCH, :] = value.astype(bf16)


def stacked(x):
    high, low = split2(x)
    return jnp.concatenate([high, low, high, jnp.zeros((32, x.shape[1]), bf16)], axis=0)


def slot(s):
    return 0 if s == 0 else 1 if s == LAYERS - 1 else 2 + s % 3


def kernel(
    lower_hbm_rows,
    upper_hbm_rows,
    phase_hbm,
    jacobian_hbm,
    u_hbm,
    metric_hbm,
    upper_hbm,
    lower_hbm,
    out,
    u,
    metric,
    upper_held,
    lower_held,
    order,
    sorted_own,
    sorted_in,
    partner_ref,
    phase_ref,
    jacobian,
    raw_in,
    basis_own,
    basis_in,
    parts,
    ghost_own,
    ghost_out,
    ghost_in,
    halo_out,
    halo,
    edge_out,
    edge_in,
    edge_add,
    fix,
    stencil,
    pitch_part,
    span_part,
    axial_part,
    small_sem,
    u_sem,
    metric_sem,
    panel_sem,
    send_sem,
    recv_sem,
):
    axial, span = lax.axis_index("axial"), lax.axis_index("span")
    axial_last, span_last = lax.axis_size("axial") - 1, lax.axis_size("span") - 1
    has_left, has_right = axial > 0, axial < axial_last
    has_down, has_up = span > 0, span < span_last
    left = {"axial": jnp.maximum(axial - 1, 0)}
    right = {"axial": jnp.minimum(axial + 1, axial_last)}
    down = {"span": jnp.maximum(span - 1, 0)}
    up = {"span": jnp.minimum(span + 1, span_last)}
    sides = ((has_left, left), (has_right, right))

    barrier = pltpu.get_barrier_semaphore()
    around = sides + ((has_down, down), (has_up, up))
    for present, device in around:

        @pl.when(present)
        def _():
            pl.semaphore_signal(barrier, inc=1, device_id=device, device_id_type=MESH)

    u_copies = [pltpu.make_async_copy(u_hbm.at[:, s], u.at[:, s], u_sem.at[s]) for s in range(LAYERS)]
    metric_copies = [
        pltpu.make_async_copy(metric_hbm.at[:, s], metric.at[:, s], metric_sem.at[s])
        for s in range(LAYERS)
    ]
    panel = (upper_held, lower_held)
    panel_copies = [
        pltpu.make_async_copy(
            hbm.at[:, t * TILE : (t + 1) * TILE], panel[i].at[t], panel_sem.at[i, t]
        )
        for i, hbm in enumerate((upper_hbm, lower_hbm))
        for t in range(TILES)
    ]
    ends, inner = [u_copies[0], u_copies[-1]], u_copies[1:-1]
    small = [
        pltpu.make_async_copy(source, target, small_sem.at[i])
        for i, (source, target) in enumerate(
            (
                (lower_hbm_rows, partner_ref.at[0]),
                (upper_hbm_rows, partner_ref.at[1]),
                (phase_hbm, phase_ref),
                (jacobian_hbm, jacobian),
            )
        )
    ]
    for c in small + ends + panel_copies[:TILES]:
        c.start()

    for i, (present, _) in enumerate(sides):

        @pl.when(jnp.logical_not(present))
        def _():
            sorted_in[i] = jnp.zeros((8, ROWS), f32)
            raw_in[i] = jnp.zeros((2, 8, 128), jnp.int32)
            ghost_in[i] = jnp.zeros((2, FS, ROWS), f32)
            edge_in[i] = jnp.zeros((FIELDS, PITCH, 128), f32)

    for i, present in enumerate((has_down, has_up)):

        @pl.when(jnp.logical_not(present))
        def _():
            halo[i] = jnp.zeros((FIELDS, PITCH, ROWS), bf16)

    for c in small:
        c.wait()
    cosine, sine = jnp.cos(phase_ref[...]), jnp.sin(phase_ref[...])
    upper_sorted = sort_rows(partner_ref[0], cosine, sine, order.at[0])
    lower_sorted = sort_rows(partner_ref[1], cosine, -sine, order.at[1])
    lines = [x for pair in zip(upper_sorted, lower_sorted) for x in pair]
    sorted_own[...] = jnp.concatenate(lines + [jnp.zeros((2, ROWS), f32)], axis=0)

    for c in panel_copies[TILES:]:
        c.start()
    for c in ends:
        c.wait()
    halo_out[0] = u[:, 0].astype(bf16)
    halo_out[1] = u[:, LAYERS - 1].astype(bf16)

    pl.semaphore_wait(barrier, sum(present.astype(jnp.int32) for present, _ in around))

    def remote(number, source, target, device):
        return pltpu.make_async_remote_copy(
            src_ref=source,
            dst_ref=target,
            send_sem=send_sem.at[number],
            recv_sem=recv_sem.at[number],
            device_id=device,
            device_id_type=MESH,
        )

    def tables(i, device):
        return [
            remote(i, sorted_own, sorted_in.at[1 - i], device),
            remote(2 + i, partner_ref, raw_in.at[1 - i], device),
        ]

    def edges(i, device):
        return remote(4 + i, edge_out.at[i], edge_in.at[1 - i], device)

    def ghosts(i, device):
        return remote(6 + i, ghost_out.at[i], ghost_in.at[1 - i], device)

    def halos(i, device):
        return remote(8 + i, halo_out.at[i], halo.at[1 - i], device)

    for i, (present, device) in enumerate(sides):

        @pl.when(present)
        def _():
            for c in tables(i, device):
                c.start()

    for i, (present, device) in enumerate(((has_down, down), (has_up, up))):

        @pl.when(present)
        def _():
            halos(i, device).start()

    fill_stencil(jacobian, stencil)
    fill_basis(sorted_own[2:4], sorted_own[4:6], basis_own)

    first_row = axial * ROWS

    for i in range(2):
        for c in panel_copies[i * TILES : (i + 1) * TILES]:
            c.wait()
        for c in (inner, metric_copies)[i]:
            c.start()
        evaluate(
            panel[i], basis_own, i, sorted_own[i : i + 1], partner_ref[i], first_row, parts,
            ghost_own.at[i],
        )

    for c in inner:
        c.wait()
    lane = lax.broadcasted_iota(jnp.int32, (PITCH, 128), 1)
    for i, (at, turn) in enumerate(((0, 0), (ROWS - 128, 1))):
        for f in range(FIELDS):
            packed = jnp.zeros((PITCH, 128), f32)
            for s in range(LAYERS):
                turned = u[f, s, :, at : at + 128]
                if (s + turn) % 128:
                    turned = pltpu.roll(turned, s + turn, 1)
                packed = jnp.where(lane == s, turned, packed)
            edge_out[i, f] = packed
    for i, (present, device) in enumerate(sides):

        @pl.when(present)
        def _():
            edges(i, device).start()

    for i, (present, device) in enumerate(sides):

        @pl.when(present)
        def _():
            for c in tables(1 - i, device):
                c.wait_recv()

    odd = axial % 2
    order_in = (odd, 1 - odd)
    fill_basis(
        jnp.concatenate([sorted_in[i, 2:4] for i in order_in], axis=0),
        jnp.concatenate([sorted_in[i, 4:6] for i in order_in], axis=0),
        basis_in,
    )
    for step, i in enumerate(order_in):
        for p in range(2):
            evaluate(
                panel[p], basis_in, 2 * step + p, sorted_in[i, p : p + 1], raw_in[i, p],
                first_row, parts, ghost_out.at[i, p],
            )
        target = axial - 1 + 2 * i

        @pl.when((target >= 0) & (target <= axial_last))
        def _():
            ghosts(i, {"axial": jnp.clip(target, 0, axial_last)}).start()

    def products(s):
        for t in range(TILES):
            at = slice(t * TILE, (t + 1) * TILE)
            x = stacked(u[:, s, :, at].reshape(FP, TILE))
            y = jnp.dot(stencil[...], x, preferred_element_type=f32)
            pitch_part[slot(s), :, at] = y[0:FP]
            span_part[s + 1, :, at] = y[FP : 2 * FP]
            axial_part[slot(s), :, at] = y[2 * FP : 3 * FP]

    def outside(i):
        for t in range(TILES):
            at = slice(t * TILE, (t + 1) * TILE)
            x = halo[i, :, :, at].reshape(FP, TILE)
            x = jnp.concatenate([x, jnp.zeros_like(x), x, jnp.zeros((32, TILE), bf16)], axis=0)
            y = jnp.dot(stencil[FP : 2 * FP, :], x, preferred_element_type=f32)
            span_part[i * (LAYERS + 1), :, at] = y

    lane8 = lax.broadcasted_iota(jnp.int32, (8, 128), 1)

    def lower_layer(f, t):
        pair = halo[0, f, 16 * (t // 2) : 16 * (t // 2) + 16, :].astype(f32)
        return pair[8 * (t % 2) : 8 * (t % 2) + 8]

    def combine(s):
        for t in range(PITCH // 8):
            r = slice(8 * t, 8 * t + 8)
            m = [metric[d, s, r, :] for d in range(3)]
            keep = 1.0 - 0.02 * (m[0] + m[1] + m[2])
            for f in range(FIELDS):
                rr = slice(PITCH * f + 8 * t, PITCH * f + 8 * t + 8)
                here = u[f, s, r, :]
                y = axial_part[slot(s), rr, :]
                after = pltpu.roll(y, ROWS - 1, 1)
                before = pltpu.roll(y - 0.02 * here, 1, 1)
                after_in = pltpu.roll(edge_add[1, f, r, :], (127 - s) % 128, 1)
                before_in = edge_add[0, f, r, :]
                if s:
                    before_in = pltpu.roll(before_in, 128 - s, 1)
                along = jnp.concatenate(
                    [
                        after[:, :128] - jnp.where(lane8 == 0, before_in, before[:, :128]),
                        after[:, 128:-128] - before[:, 128:-128],
                        jnp.where(lane8 == 127, after_in, after[:, -128:]) - before[:, -128:],
                    ],
                    axis=1,
                )
                lower = u[f, s - 1, r, :] if s else lower_layer(f, t)
                across = span_part[s + 2, rr, :] - span_part[s, rr, :] + 0.02 * lower
                out[f, s, r, :] = (
                    keep * here + m[2] * pitch_part[slot(s), rr, :] + m[1] * across + m[0] * along
                )

    def patch(s):
        for f in range(FIELDS):
            for i, p in enumerate((0, PITCH - 1)):
                out[f, s, p : p + 1, :] = out[f, s, p : p + 1, :] + fix[i, f, s : s + 1, :]

    for c in metric_copies:
        c.wait()
    products(0)
    products(1)

    for i, (present, device) in enumerate(sides):

        @pl.when(present)
        def _():
            edges(1 - i, device).wait_recv()

    for i, (present, device) in enumerate(((has_down, down), (has_up, up))):

        @pl.when(present)
        def _():
            halos(1 - i, device).wait_recv()

    for i, sign in ((0, -0.01), (1, 0.01)):
        for f in range(FIELDS):
            total = sign * edge_in[i, f]
            for g in range(FIELDS):
                total = total + (-0.1 * jacobian[f, 0, g]) * edge_in[i, g]
            edge_add[i, f] = total

    outside(0)
    outside(1)
    combine(0)
    for s in range(2, 6):
        products(s)
        combine(s - 1)

    for i, (present, device) in enumerate(sides):

        @pl.when(present)
        def _():
            ghosts(1 - i, device).wait_recv()

    for i, (p, sign) in enumerate(((0, 0.1), (PITCH - 1, -0.1))):
        total = ghost_own[i] + ghost_in[0, i] + ghost_in[1, i]
        high, low = split2(total)
        both = jnp.dot(
            jnp.concatenate([high, low], axis=0), order[i], preferred_element_type=f32
        )
        ghost = both[0:FS] + both[FS : 2 * FS]
        scale = jnp.concatenate([metric[2, s, p : p + 1, :] for s in range(LAYERS)], axis=0)
        for f in range(FIELDS):
            total = 0.01 * ghost[f * LAYERS : (f + 1) * LAYERS]
            for g in range(FIELDS):
                total = total + (sign * jacobian[f, 2, g]) * ghost[g * LAYERS : (g + 1) * LAYERS]
            fix[i, f] = scale * total
        products(6 + i)
        combine(5 + i)
    combine(LAYERS - 1)
    for s in range(LAYERS):
        patch(s)

    for i, (present, device) in enumerate(sides):

        @pl.when(present)
        def _():
            for c in tables(i, device) + [edges(i, device), ghosts(i, device)]:
                c.wait_send()

    for i, (present, device) in enumerate(((has_down, down), (has_up, up))):

        @pl.when(present)
        def _():
            halos(i, device).wait_send()


def store(held, out, sems):
    copies = [
        pltpu.make_async_copy(held.at[:, s], out.at[:, s], sems.at[s]) for s in range(LAYERS)
    ]
    for c in copies:
        c.start()
    for c in copies:
        c.wait()


def on_device(
    conserved, metric, jacobian, upper_panel, lower_panel, lower_partner, upper_partner, lag_phase
):
    rows = [x.reshape(8, 128) for x in (lower_partner, upper_partner, lag_phase)]
    jacobian = jnp.transpose(jacobian, (1, 0, 2))
    upper = upper_panel.reshape(MODES * FS, ROWS)
    lower = lower_panel.reshape(MODES * FS, ROWS)
    vmem = pl.BlockSpec(memory_space=pltpu.VMEM)
    anywhere = pl.BlockSpec(memory_space=pl.ANY)
    shape = (FIELDS, LAYERS, PITCH, ROWS)
    advanced = pl.pallas_call(
        kernel,
        out_shape=pltpu.VMEM(shape, f32),
        in_specs=[anywhere] * 8,
        out_specs=vmem,
        scratch_shapes=[
            pltpu.VMEM(shape, f32),
            pltpu.VMEM((3, LAYERS, PITCH, ROWS), f32),
            pltpu.VMEM((TILES, MODES * FS, TILE), bf16),
            pltpu.VMEM((TILES, MODES * FS, TILE), bf16),
            pltpu.VMEM((2, ROWS, ROWS), bf16),
            pltpu.VMEM((8, ROWS), f32),
            pltpu.VMEM((2, 8, ROWS), f32),
            pltpu.VMEM((2, 8, 128), jnp.int32),
            pltpu.VMEM((8, 128), f32),
            pltpu.SMEM((FIELDS, 3, FIELDS), f32),
            pltpu.VMEM((2, 2, 8, 128), jnp.int32),
            pltpu.VMEM((TILES, MODES, 8, TILE), f32),
            pltpu.VMEM((TILES, MODES, 8, TILE), f32),
            pltpu.VMEM((PAIRS, FS, TILE), f32),
            pltpu.VMEM((2, FS, ROWS), f32),
            pltpu.VMEM((2, 2, FS, ROWS), f32),
            pltpu.VMEM((2, 2, FS, ROWS), f32),
            pltpu.VMEM((2, FIELDS, PITCH, ROWS), bf16),
            pltpu.VMEM((2, FIELDS, PITCH, ROWS), bf16),
            pltpu.VMEM((2, FIELDS, PITCH, 128), f32),
            pltpu.VMEM((2, FIELDS, PITCH, 128), f32),
            pltpu.VMEM((2, FIELDS, PITCH, 128), f32),
            pltpu.VMEM((2, FIELDS, LAYERS, ROWS), f32),
            pltpu.VMEM((3 * FP, 512), bf16),
            pltpu.VMEM((5, FP, ROWS), f32),
            pltpu.VMEM((LAYERS + 2, FP, ROWS), f32),
            pltpu.VMEM((5, FP, ROWS), f32),
            pltpu.SemaphoreType.DMA((4,)),
            pltpu.SemaphoreType.DMA((LAYERS,)),
            pltpu.SemaphoreType.DMA((LAYERS,)),
            pltpu.SemaphoreType.DMA((2, TILES)),
            pltpu.SemaphoreType.DMA((10,)),
            pltpu.SemaphoreType.DMA((10,)),
        ],
        compiler_params=pltpu.CompilerParams(
            collective_id=0, has_side_effects=True, vmem_limit_bytes=50 * 2**20
        ),
        name="section",
    )(*rows, jacobian, conserved, metric, upper, lower)
    return pl.pallas_call(
        store,
        out_shape=jax.ShapeDtypeStruct(shape, f32),
        in_specs=[vmem],
        out_specs=anywhere,
        scratch_shapes=[pltpu.SemaphoreType.DMA((LAYERS,))],
        compiler_params=pltpu.CompilerParams(vmem_limit_bytes=4 * 2**20),
        name="store",
    )(pltpu.with_memory_space_constraint(advanced, pltpu.VMEM))


def solution(mesh):
    in_specs = (
        P(None, "span", None, "axial"),
        P(None, "span", None, "axial"),
        P(),
        P(None, None, "span", "axial"),
        P(None, None, "span", "axial"),
        P("axial"),
        P("axial"),
        P("axial"),
    )
    out_specs = P(None, "span", None, "axial")
    return jax.shard_map(
        on_device, mesh=mesh, in_specs=in_specs, out_specs=out_specs, check_vma=False
    )
```

```python
import functools

import jax
import jax.numpy as jnp
from jax import lax
from jax.experimental import pallas as pl
from jax.experimental.pallas import tpu as pltpu
from jax.sharding import PartitionSpec as P

f32 = jnp.float32
bf16 = jnp.bfloat16
MESH = pl.DeviceIdType.MESH

FIELDS = 5
LAYERS = 8
PITCH = 32
ROWS = 1024
MODES = 32
FS = FIELDS * LAYERS
FP = FIELDS * PITCH
HALF = PITCH // 2
TILE = 256
TILES = ROWS // TILE
PAIRS = 2 * TILES - 1
OWN, LEFT, RIGHT = 0, 1, 2


def row_of(x):
    return jnp.concatenate([x[r : r + 1, :] for r in range(8)], axis=1)


def split2(x):
    high = x.astype(bf16)
    return high, (x - high.astype(f32)).astype(bf16)


def split3(x):
    high = x.astype(bf16).astype(f32)
    rest = x - high
    middle = rest.astype(bf16).astype(f32)
    return [high, middle, rest - middle]


def one_hot(places):
    inside = (places >= 0.0) & (places < TILE)
    wanted = jnp.where(inside, places, -1.0).astype(bf16)
    out = []
    for j in range(places.shape[1] // TILE):
        k = lax.broadcasted_iota(jnp.int32, (TILE, TILE), 0).astype(bf16)
        w = wanted[:, j * TILE : (j + 1) * TILE]
        out.append(jnp.where(k == w, bf16(1), bf16(0)))
    return out


def sort_rows(partner, cosine, sine, order):
    index = lax.broadcasted_iota(jnp.int32, (8, 128), 0) * 128 + lax.broadcasted_iota(
        jnp.int32, (8, 128), 1
    )
    key = (partner * ROWS + index).astype(f32)
    counts = [jnp.zeros((8, 128), f32) for _ in range(8)]
    for c in range(8):
        column = jnp.transpose(jnp.broadcast_to(key[c : c + 1, :], (128, 128)))
        for r in range(8):
            less = jnp.where(column < key[r : r + 1, :], 1.0, 0.0)
            counts[r] = counts[r] + jnp.sum(less.reshape(16, 8, 128), axis=0)
    rank = jnp.concatenate([jnp.sum(c, axis=0, keepdims=True) for c in counts], axis=1)
    for t in range(TILES):
        for j, block in enumerate(one_hot(rank - float(t * TILE))):
            order[t * TILE : (t + 1) * TILE, j * TILE : (j + 1) * TILE] = block
    pieces = [(partner // 256).astype(f32), (partner % 256).astype(f32)]
    pieces += split3(cosine) + split3(sine)
    values = jnp.concatenate([row_of(x) for x in pieces] + [jnp.zeros((8, ROWS), f32)], axis=0)
    placed = lax.dot_general(
        values.astype(bf16), order[...], (((1,), (1,)), ((), ())), preferred_element_type=f32
    )
    return (
        placed[0:1] * 256.0 + placed[1:2],
        (placed[4:5] + placed[3:4]) + placed[2:3],
        (placed[7:8] + placed[6:7]) + placed[5:6],
    )


def fill_basis(cosine, sine, basis):
    c, s = jnp.ones_like(cosine), jnp.zeros_like(sine)
    n = cosine.shape[0]
    for k in range(MODES // 2):
        for j in range(TILES):
            basis[j, 2 * k, 0:n, :] = c[:, j * TILE : (j + 1) * TILE]
            basis[j, 2 * k + 1, 0:n, :] = s[:, j * TILE : (j + 1) * TILE]
        c, s = c * cosine - s * sine, s * cosine + c * sine


def evaluate(panel, basis, line, sorted_row, raw, first_row, parts, ghost):
    bounds = [jnp.sum((raw < first_row + t * TILE).astype(jnp.int32)) for t in range(TILES + 1)]
    start = first_row.astype(f32)
    tile = jnp.int32(0)
    block = jnp.minimum(bounds[0] // TILE, TILES - 1)
    blocks = []
    for i in range(PAIRS):
        used = jnp.minimum(tile, TILES - 1)
        row = sorted_row[:, 0:TILE]
        for j in range(1, TILES):
            row = jnp.where(block == j, sorted_row[:, j * TILE : (j + 1) * TILE], row)
        shift = jnp.where(tile < TILES, (tile * TILE).astype(f32), 1.0e6)
        chosen = one_hot(row - (start + shift))[0]
        total = None
        half = MODES // 2
        for h in range(2):
            picked = jnp.dot(
                panel[used, h * half * FS : (h + 1) * half * FS, :],
                chosen,
                preferred_element_type=f32,
            )
            for m in range(half):
                weight = basis[block, h * half + m, line : line + 1, :]
                term = picked[m * FS : (m + 1) * FS] * weight
                total = term if total is None else total + term
        parts[i] = total
        blocks.append(block)
        end = bounds[TILES]
        for t in range(TILES - 1, 0, -1):
            end = jnp.where(tile == t - 1, bounds[t], end)
        over = (end > (block + 1) * TILE) & (block < TILES - 1) & (tile < TILES)
        tile = jnp.where(over, tile, tile + 1)
        block = jnp.where(over, block + 1, block)
    for j in range(TILES):
        total = jnp.zeros((FS, TILE), f32)
        for i in range(PAIRS):
            total = total + parts[i] * (blocks[i] == j).astype(f32)
        ghost[:, j * TILE : (j + 1) * TILE] = total


def fill_stencil(jacobian, directions, cells, stencil):
    width = stencil.shape[1]
    size = FIELDS * cells
    column = lax.broadcasted_iota(jnp.int32, (cells, width), 1)
    row = lax.broadcasted_iota(jnp.int32, (cells, width), 0)
    third = jnp.where(
        column < size, 0, jnp.where(column < 2 * size, 1, jnp.where(column < 3 * size, 2, 3))
    )
    place = column - size * third
    field = jnp.where(third < 3, place // cells, -1)
    cell = place % cells
    here = cell == row
    above = cell == row + 1
    below = cell == row - 1
    for block, d in enumerate(directions):
        for f in range(FIELDS):
            weight = jnp.zeros((cells, width), f32)
            for g in range(FIELDS):
                weight = jnp.where(field == g, -0.1 * jacobian[f, d, g], weight)
            weight = jnp.where(third < 3, weight, 0.0)
            smooth = jnp.where(field == f, f32(0.01), f32(0.0))
            if d == 2:
                value = jnp.where(above, smooth + weight, jnp.where(below, smooth - weight, 0.0))
            else:
                value = jnp.where(here, smooth + weight, 0.0)
            high = value.astype(bf16).astype(f32)
            value = jnp.where(third == 2, value - high, high)
            at = (block * FIELDS + f) * cells
            stencil[at : at + cells, :] = value.astype(bf16)


def stacked(high, low, first, cells):
    def part(x):
        return [x[PITCH * g + first : PITCH * g + first + cells] for g in range(FIELDS)]

    pad = -3 * FIELDS * cells % TILE
    rows = part(high) + part(low) + part(high) + [jnp.zeros((pad, high.shape[1]), bf16)]
    return jnp.concatenate(rows, axis=0)


def slot(s):
    return 0 if s == 0 else 1 if s == LAYERS - 1 else 2 + s % 3


def kernel(
    lower_hbm_rows,
    upper_hbm_rows,
    phase_hbm,
    jacobian_hbm,
    u_hbm,
    metric_hbm,
    upper_hbm,
    lower_hbm,
    out,
    u,
    metric,
    upper_held,
    lower_held,
    order,
    sorted_own,
    sorted_in,
    partner_ref,
    phase_ref,
    jacobian,
    raw_in,
    basis_own,
    basis_in,
    parts,
    ghost_own,
    ghost_out,
    ghost_in,
    halo_out,
    halo,
    edge_out,
    edge_in,
    edge_add,
    fix,
    pitch_matrix,
    side_matrix,
    pitch_part,
    span_part,
    axial_part,
    small_sem,
    u_sem,
    metric_sem,
    panel_sem,
    send_sem,
    recv_sem,
):
    axial, span = lax.axis_index("axial"), lax.axis_index("span")
    axial_last, span_last = lax.axis_size("axial") - 1, lax.axis_size("span") - 1
    has_left, has_right = axial > 0, axial < axial_last
    has_down, has_up = span > 0, span < span_last
    left = {"axial": jnp.maximum(axial - 1, 0)}
    right = {"axial": jnp.minimum(axial + 1, axial_last)}
    down = {"span": jnp.maximum(span - 1, 0)}
    up = {"span": jnp.minimum(span + 1, span_last)}
    sides = ((has_left, left), (has_right, right))

    barrier = pltpu.get_barrier_semaphore()
    around = sides + ((has_down, down), (has_up, up))
    for present, device in around:

        @pl.when(present)
        def _():
            pl.semaphore_signal(barrier, inc=1, device_id=device, device_id_type=MESH)

    u_copies = [pltpu.make_async_copy(u_hbm.at[:, s], u.at[:, s], u_sem.at[s]) for s in range(LAYERS)]
    metric_copies = [
        pltpu.make_async_copy(metric_hbm.at[:, s], metric.at[:, s], metric_sem.at[s])
        for s in range(LAYERS)
    ]
    panel = (upper_held, lower_held)
    panel_copies = [
        pltpu.make_async_copy(
            hbm.at[:, t * TILE : (t + 1) * TILE], panel[i].at[t], panel_sem.at[i, t]
        )
        for i, hbm in enumerate((upper_hbm, lower_hbm))
        for t in range(TILES)
    ]
    ends, inner = [u_copies[0], u_copies[-1]], u_copies[1:-1]
    small = [
        pltpu.make_async_copy(source, target, small_sem.at[i])
        for i, (source, target) in enumerate(
            (
                (lower_hbm_rows, partner_ref.at[0]),
                (upper_hbm_rows, partner_ref.at[1]),
                (phase_hbm, phase_ref),
                (jacobian_hbm, jacobian),
            )
        )
    ]
    for c in small + ends + panel_copies[:TILES]:
        c.start()

    for i, (present, _) in enumerate(sides):

        @pl.when(jnp.logical_not(present))
        def _():
            sorted_in[i] = jnp.zeros((8, ROWS), f32)
            raw_in[i] = jnp.zeros((2, 8, 128), jnp.int32)
            ghost_in[i] = jnp.zeros((2, FS, ROWS), f32)
            edge_in[i] = jnp.zeros((FIELDS, PITCH, 128), f32)

    for i, present in enumerate((has_down, has_up)):

        @pl.when(jnp.logical_not(present))
        def _():
            halo[i] = jnp.zeros((FIELDS, PITCH, ROWS), bf16)

    for c in small:
        c.wait()
    cosine, sine = jnp.cos(phase_ref[...]), jnp.sin(phase_ref[...])
    upper_sorted = sort_rows(partner_ref[0], cosine, sine, order.at[0])
    lower_sorted = sort_rows(partner_ref[1], cosine, -sine, order.at[1])
    lines = [x for pair in zip(upper_sorted, lower_sorted) for x in pair]
    sorted_own[...] = jnp.concatenate(lines + [jnp.zeros((2, ROWS), f32)], axis=0)

    for c in panel_copies[TILES:]:
        c.start()
    for c in ends:
        c.wait()
    halo_out[0] = u[:, 0].astype(bf16)
    halo_out[1] = u[:, LAYERS - 1].astype(bf16)

    pl.semaphore_wait(barrier, sum(present.astype(jnp.int32) for present, _ in around))

    def remote(number, source, target, device):
        return pltpu.make_async_remote_copy(
            src_ref=source,
            dst_ref=target,
            send_sem=send_sem.at[number],
            recv_sem=recv_sem.at[number],
            device_id=device,
            device_id_type=MESH,
        )

    def tables(i, device):
        return [
            remote(i, sorted_own, sorted_in.at[1 - i], device),
            remote(2 + i, partner_ref, raw_in.at[1 - i], device),
        ]

    def edges(i, device):
        return remote(4 + i, edge_out.at[i], edge_in.at[1 - i], device)

    def ghosts(i, device):
        return remote(6 + i, ghost_out.at[i], ghost_in.at[1 - i], device)

    def halos(i, device):
        return remote(8 + i, halo_out.at[i], halo.at[1 - i], device)

    for i, (present, device) in enumerate(sides):

        @pl.when(present)
        def _():
            for c in tables(i, device):
                c.start()

    for i, (present, device) in enumerate(((has_down, down), (has_up, up))):

        @pl.when(present)
        def _():
            halos(i, device).start()

    fill_stencil(jacobian, (2,), PITCH, pitch_matrix)
    fill_stencil(jacobian, (1, 0), HALF, side_matrix)
    fill_basis(sorted_own[2:4], sorted_own[4:6], basis_own)

    first_row = axial * ROWS

    for i in range(2):
        for c in panel_copies[i * TILES : (i + 1) * TILES]:
            c.wait()
        for c in (inner, metric_copies)[i]:
            c.start()
        evaluate(
            panel[i], basis_own, i, sorted_own[i : i + 1], partner_ref[i], first_row, parts,
            ghost_own.at[i],
        )

    for c in inner:
        c.wait()
    lane = lax.broadcasted_iota(jnp.int32, (PITCH, 128), 1)
    for i, (at, turn) in enumerate(((0, 0), (ROWS - 128, 1))):
        for f in range(FIELDS):
            packed = jnp.zeros((PITCH, 128), f32)
            for s in range(LAYERS):
                turned = u[f, s, :, at : at + 128]
                if (s + turn) % 128:
                    turned = pltpu.roll(turned, s + turn, 1)
                packed = jnp.where(lane == s, turned, packed)
            edge_out[i, f] = packed
    for i, (present, device) in enumerate(sides):

        @pl.when(present)
        def _():
            edges(i, device).start()

    for i, (present, device) in enumerate(sides):

        @pl.when(present)
        def _():
            for c in tables(1 - i, device):
                c.wait_recv()

    odd = axial % 2
    order_in = (odd, 1 - odd)
    fill_basis(
        jnp.concatenate([sorted_in[i, 2:4] for i in order_in], axis=0),
        jnp.concatenate([sorted_in[i, 4:6] for i in order_in], axis=0),
        basis_in,
    )
    for step, i in enumerate(order_in):
        for p in range(2):
            evaluate(
                panel[p], basis_in, 2 * step + p, sorted_in[i, p : p + 1], raw_in[i, p],
                first_row, parts, ghost_out.at[i, p],
            )
        target = axial - 1 + 2 * i

        @pl.when((target >= 0) & (target <= axial_last))
        def _():
            ghosts(i, {"axial": jnp.clip(target, 0, axial_last)}).start()

    def products(s):
        for t in range(TILES):
            at = slice(t * TILE, (t + 1) * TILE)
            high, low = split2(u[:, s, :, at].reshape(FP, TILE))
            x = stacked(high, low, 0, PITCH)
            pitch_part[slot(s), :, at] = jnp.dot(
                pitch_matrix[...], x, preferred_element_type=f32
            )
            for first in (0, HALF):
                x = stacked(high, low, first, HALF)
                y = jnp.dot(side_matrix[...], x, preferred_element_type=f32)
                for f in range(FIELDS):
                    r = slice(PITCH * f + first, PITCH * f + first + HALF)
                    span_part[s + 1, r, at] = y[HALF * f : HALF * (f + 1)]
                    axial_part[slot(s), r, at] = y[HALF * (FIELDS + f) : HALF * (FIELDS + f + 1)]

    def outside(i):
        for t in range(TILES):
            at = slice(t * TILE, (t + 1) * TILE)
            high = halo[i, :, :, at].reshape(FP, TILE)
            for first in (0, HALF):
                x = stacked(high, jnp.zeros_like(high), first, HALF)
                y = jnp.dot(
                    side_matrix[0 : FIELDS * HALF, :], x, preferred_element_type=f32
                )
                for f in range(FIELDS):
                    r = slice(PITCH * f + first, PITCH * f + first + HALF)
                    span_part[i * (LAYERS + 1), r, at] = y[HALF * f : HALF * (f + 1)]

    lane8 = lax.broadcasted_iota(jnp.int32, (8, 128), 1)

    def lower_layer(f, t):
        pair = halo[0, f, 16 * (t // 2) : 16 * (t // 2) + 16, :].astype(f32)
        return pair[8 * (t % 2) : 8 * (t % 2) + 8]

    def combine(s):
        for t in range(PITCH // 8):
            r = slice(8 * t, 8 * t + 8)
            m = [metric[d, s, r, :] for d in range(3)]
            keep = 1.0 - 0.02 * (m[0] + m[1] + m[2])
            for f in range(FIELDS):
                rr = slice(PITCH * f + 8 * t, PITCH * f + 8 * t + 8)
                here = u[f, s, r, :]
                y = axial_part[slot(s), rr, :]
                after = pltpu.roll(y, ROWS - 1, 1)
                before = pltpu.roll(y - 0.02 * here, 1, 1)
                after_in = pltpu.roll(edge_add[1, f, r, :], (127 - s) % 128, 1)
                before_in = edge_add[0, f, r, :]
                if s:
                    before_in = pltpu.roll(before_in, 128 - s, 1)
                along = jnp.concatenate(
                    [
                        after[:, :128] - jnp.where(lane8 == 0, before_in, before[:, :128]),
                        after[:, 128:-128] - before[:, 128:-128],
                        jnp.where(lane8 == 127, after_in, after[:, -128:]) - before[:, -128:],
                    ],
                    axis=1,
                )
                lower = u[f, s - 1, r, :] if s else lower_layer(f, t)
                across = span_part[s + 2, rr, :] - span_part[s, rr, :] + 0.02 * lower
                out[f, s, r, :] = (
                    keep * here + m[2] * pitch_part[slot(s), rr, :] + m[1] * across + m[0] * along
                )

    def patch(s):
        for f in range(FIELDS):
            for i, p in enumerate((0, PITCH - 1)):
                out[f, s, p : p + 1, :] = out[f, s, p : p + 1, :] + fix[i, f, s : s + 1, :]

    for c in metric_copies:
        c.wait()
    products(0)
    products(1)

    for i, (present, device) in enumerate(sides):

        @pl.when(present)
        def _():
            edges(1 - i, device).wait_recv()

    for i, sign in ((0, -0.01), (1, 0.01)):
        for f in range(FIELDS):
            total = sign * edge_in[i, f]
            for g in range(FIELDS):
                total = total + (-0.1 * jacobian[f, 0, g]) * edge_in[i, g]
            edge_add[i, f] = total

    for s in range(2, 6):
        products(s)
        combine(s - 1)

    for i, (present, device) in enumerate(sides):

        @pl.when(present)
        def _():
            ghosts(1 - i, device).wait_recv()

    for i, (present, device) in enumerate(((has_down, down), (has_up, up))):

        @pl.when(present)
        def _():
            halos(1 - i, device).wait_recv()

    for i, (p, sign) in enumerate(((0, 0.1), (PITCH - 1, -0.1))):
        total = ghost_own[i] + ghost_in[0, i] + ghost_in[1, i]
        high, low = split2(total)
        both = jnp.dot(
            jnp.concatenate([high, low], axis=0), order[i], preferred_element_type=f32
        )
        ghost = both[0:FS] + both[FS : 2 * FS]
        scale = jnp.concatenate([metric[2, s, p : p + 1, :] for s in range(LAYERS)], axis=0)
        for f in range(FIELDS):
            total = 0.01 * ghost[f * LAYERS : (f + 1) * LAYERS]
            for g in range(FIELDS):
                total = total + (sign * jacobian[f, 2, g]) * ghost[g * LAYERS : (g + 1) * LAYERS]
            fix[i, f] = scale * total
        outside(i)
        products(6 + i)
        combine(5 + i)
    combine(0)
    combine(LAYERS - 1)
    for s in range(LAYERS):
        patch(s)

    for i, (present, device) in enumerate(sides):

        @pl.when(present)
        def _():
            for c in tables(i, device) + [edges(i, device), ghosts(i, device)]:
                c.wait_send()

    for i, (present, device) in enumerate(((has_down, down), (has_up, up))):

        @pl.when(present)
        def _():
            halos(i, device).wait_send()


def store(held, out, sems):
    copies = [
        pltpu.make_async_copy(held.at[:, s], out.at[:, s], sems.at[s]) for s in range(LAYERS)
    ]
    for c in copies:
        c.start()
    for c in copies:
        c.wait()


def on_device(
    conserved, metric, jacobian, upper_panel, lower_panel, lower_partner, upper_partner, lag_phase
):
    rows = [x.reshape(8, 128) for x in (lower_partner, upper_partner, lag_phase)]
    jacobian = jnp.transpose(jacobian, (1, 0, 2))
    upper = upper_panel.reshape(MODES * FS, ROWS)
    lower = lower_panel.reshape(MODES * FS, ROWS)
    vmem = pl.BlockSpec(memory_space=pltpu.VMEM)
    anywhere = pl.BlockSpec(memory_space=pl.ANY)
    shape = (FIELDS, LAYERS, PITCH, ROWS)
    advanced = pl.pallas_call(
        kernel,
        out_shape=pltpu.VMEM(shape, f32),
        in_specs=[anywhere] * 8,
        out_specs=vmem,
        scratch_shapes=[
            pltpu.VMEM(shape, f32),
            pltpu.VMEM((3, LAYERS, PITCH, ROWS), f32),
            pltpu.VMEM((TILES, MODES * FS, TILE), bf16),
            pltpu.VMEM((TILES, MODES * FS, TILE), bf16),
            pltpu.VMEM((2, ROWS, ROWS), bf16),
            pltpu.VMEM((8, ROWS), f32),
            pltpu.VMEM((2, 8, ROWS), f32),
            pltpu.VMEM((2, 8, 128), jnp.int32),
            pltpu.VMEM((8, 128), f32),
            pltpu.SMEM((FIELDS, 3, FIELDS), f32),
            pltpu.VMEM((2, 2, 8, 128), jnp.int32),
            pltpu.VMEM((TILES, MODES, 8, TILE), f32),
            pltpu.VMEM((TILES, MODES, 8, TILE), f32),
            pltpu.VMEM((PAIRS, FS, TILE), f32),
            pltpu.VMEM((2, FS, ROWS), f32),
            pltpu.VMEM((2, 2, FS, ROWS), f32),
            pltpu.VMEM((2, 2, FS, ROWS), f32),
            pltpu.VMEM((2, FIELDS, PITCH, ROWS), bf16),
            pltpu.VMEM((2, FIELDS, PITCH, ROWS), bf16),
            pltpu.VMEM((2, FIELDS, PITCH, 128), f32),
            pltpu.VMEM((2, FIELDS, PITCH, 128), f32),
            pltpu.VMEM((2, FIELDS, PITCH, 128), f32),
            pltpu.VMEM((2, FIELDS, LAYERS, ROWS), f32),
            pltpu.VMEM((FP, 512), bf16),
            pltpu.VMEM((2 * FIELDS * HALF, TILE), bf16),
            pltpu.VMEM((5, FP, ROWS), f32),
            pltpu.VMEM((LAYERS + 2, FP, ROWS), f32),
            pltpu.VMEM((5, FP, ROWS), f32),
            pltpu.SemaphoreType.DMA((4,)),
            pltpu.SemaphoreType.DMA((LAYERS,)),
            pltpu.SemaphoreType.DMA((LAYERS,)),
            pltpu.SemaphoreType.DMA((2, TILES)),
            pltpu.SemaphoreType.DMA((10,)),
            pltpu.SemaphoreType.DMA((10,)),
        ],
        compiler_params=pltpu.CompilerParams(
            collective_id=0, has_side_effects=True, vmem_limit_bytes=50 * 2**20
        ),
        name="section",
    )(*rows, jacobian, conserved, metric, upper, lower)
    return pl.pallas_call(
        store,
        out_shape=jax.ShapeDtypeStruct(shape, f32),
        in_specs=[vmem],
        out_specs=anywhere,
        scratch_shapes=[pltpu.SemaphoreType.DMA((LAYERS,))],
        compiler_params=pltpu.CompilerParams(vmem_limit_bytes=4 * 2**20),
        name="store",
    )(pltpu.with_memory_space_constraint(advanced, pltpu.VMEM))


def solution(mesh):
    in_specs = (
        P(None, "span", None, "axial"),
        P(None, "span", None, "axial"),
        P(),
        P(None, None, "span", "axial"),
        P(None, None, "span", "axial"),
        P("axial"),
        P("axial"),
        P("axial"),
    )
    out_specs = P(None, "span", None, "axial")
    return jax.shard_map(
        on_device, mesh=mesh, in_specs=in_specs, out_specs=out_specs, check_vma=False
    )
```

```python
import functools

import jax
import jax.numpy as jnp
from jax import lax
from jax.experimental import pallas as pl
from jax.experimental.pallas import tpu as pltpu
from jax.sharding import PartitionSpec as P

f32 = jnp.float32
bf16 = jnp.bfloat16
MESH = pl.DeviceIdType.MESH

FIELDS = 5
LAYERS = 8
PITCH = 32
ROWS = 1024
MODES = 32
FS = FIELDS * LAYERS
FP = FIELDS * PITCH
HALF = PITCH // 2
TILE = 256
TILES = ROWS // TILE
PAIRS = 2 * TILES - 1
OWN, LEFT, RIGHT = 0, 1, 2


def row_of(x):
    return jnp.concatenate([x[r : r + 1, :] for r in range(8)], axis=1)


def split2(x):
    high = x.astype(bf16)
    return high, (x - high.astype(f32)).astype(bf16)


def split3(x):
    high = x.astype(bf16).astype(f32)
    rest = x - high
    middle = rest.astype(bf16).astype(f32)
    return [high, middle, rest - middle]


def one_hot(places):
    inside = (places >= 0.0) & (places < TILE)
    wanted = jnp.where(inside, places, -1.0).astype(bf16)
    out = []
    for j in range(places.shape[1] // TILE):
        k = lax.broadcasted_iota(jnp.int32, (TILE, TILE), 0).astype(bf16)
        w = wanted[:, j * TILE : (j + 1) * TILE]
        out.append(jnp.where(k == w, bf16(1), bf16(0)))
    return out


def sort_rows(partner, cosine, sine, order):
    index = lax.broadcasted_iota(jnp.int32, (8, 128), 0) * 128 + lax.broadcasted_iota(
        jnp.int32, (8, 128), 1
    )
    key = (partner * ROWS + index).astype(f32)
    counts = [jnp.zeros((8, 128), f32) for _ in range(8)]
    for c in range(8):
        column = jnp.transpose(jnp.broadcast_to(key[c : c + 1, :], (128, 128)))
        for r in range(8):
            less = jnp.where(column < key[r : r + 1, :], 1.0, 0.0)
            counts[r] = counts[r] + jnp.sum(less.reshape(16, 8, 128), axis=0)
    rank = jnp.concatenate([jnp.sum(c, axis=0, keepdims=True) for c in counts], axis=1)
    for t in range(TILES):
        for j, block in enumerate(one_hot(rank - float(t * TILE))):
            order[t * TILE : (t + 1) * TILE, j * TILE : (j + 1) * TILE] = block
    pieces = [(partner // 256).astype(f32), (partner % 256).astype(f32)]
    pieces += split3(cosine) + split3(sine)
    values = jnp.concatenate([row_of(x) for x in pieces] + [jnp.zeros((8, ROWS), f32)], axis=0)
    placed = lax.dot_general(
        values.astype(bf16), order[...], (((1,), (1,)), ((), ())), preferred_element_type=f32
    )
    return (
        placed[0:1] * 256.0 + placed[1:2],
        (placed[4:5] + placed[3:4]) + placed[2:3],
        (placed[7:8] + placed[6:7]) + placed[5:6],
    )


def fill_basis(cosine, sine, basis):
    c, s = jnp.ones_like(cosine), jnp.zeros_like(sine)
    n = cosine.shape[0]
    for k in range(MODES // 2):
        for j in range(TILES):
            basis[j, 2 * k, 0:n, :] = c[:, j * TILE : (j + 1) * TILE]
            basis[j, 2 * k + 1, 0:n, :] = s[:, j * TILE : (j + 1) * TILE]
        c, s = c * cosine - s * sine, s * cosine + c * sine


def evaluate(panel, basis, line, sorted_row, raw, first_row, parts, ghost):
    bounds = [jnp.sum((raw < first_row + t * TILE).astype(jnp.int32)) for t in range(TILES + 1)]
    start = first_row.astype(f32)
    tile = jnp.int32(0)
    block = jnp.minimum(bounds[0] // TILE, TILES - 1)
    blocks = []
    for i in range(PAIRS):
        used = jnp.minimum(tile, TILES - 1)
        row = sorted_row[:, 0:TILE]
        for j in range(1, TILES):
            row = jnp.where(block == j, sorted_row[:, j * TILE : (j + 1) * TILE], row)
        shift = jnp.where(tile < TILES, (tile * TILE).astype(f32), 1.0e6)
        chosen = one_hot(row - (start + shift))[0]
        total = None
        half = MODES // 2
        for h in range(2):
            picked = jnp.dot(
                panel[used, h * half * FS : (h + 1) * half * FS, :],
                chosen,
                preferred_element_type=f32,
            )
            for m in range(half):
                weight = basis[block, h * half + m, line : line + 1, :]
                term = picked[m * FS : (m + 1) * FS] * weight
                total = term if total is None else total + term
        parts[i] = total
        blocks.append(block)
        end = bounds[TILES]
        for t in range(TILES - 1, 0, -1):
            end = jnp.where(tile == t - 1, bounds[t], end)
        over = (end > (block + 1) * TILE) & (block < TILES - 1) & (tile < TILES)
        tile = jnp.where(over, tile, tile + 1)
        block = jnp.where(over, block + 1, block)
    for j in range(TILES):
        total = jnp.zeros((FS, TILE), f32)
        for i in range(PAIRS):
            total = total + parts[i] * (blocks[i] == j).astype(f32)
        ghost[:, j * TILE : (j + 1) * TILE] = total


def fill_stencil(jacobian, directions, cells, stencil):
    width = stencil.shape[1]
    size = FIELDS * cells
    column = lax.broadcasted_iota(jnp.int32, (cells, width), 1)
    row = lax.broadcasted_iota(jnp.int32, (cells, width), 0)
    third = jnp.where(
        column < size, 0, jnp.where(column < 2 * size, 1, jnp.where(column < 3 * size, 2, 3))
    )
    place = column - size * third
    field = jnp.where(third < 3, place // cells, -1)
    cell = place % cells
    here = cell == row
    above = cell == row + 1
    below = cell == row - 1
    for block, d in enumerate(directions):
        for f in range(FIELDS):
            weight = jnp.zeros((cells, width), f32)
            for g in range(FIELDS):
                weight = jnp.where(field == g, -0.1 * jacobian[f, d, g], weight)
            weight = jnp.where(third < 3, weight, 0.0)
            smooth = jnp.where(field == f, f32(0.01), f32(0.0))
            if d == 2:
                value = jnp.where(above, smooth + weight, jnp.where(below, smooth - weight, 0.0))
            else:
                value = jnp.where(here, smooth + weight, 0.0)
            high = value.astype(bf16).astype(f32)
            value = jnp.where(third == 2, value - high, high)
            at = (block * FIELDS + f) * cells
            stencil[at : at + cells, :] = value.astype(bf16)


def stacked(high, low, first, cells):
    def part(x):
        return [x[PITCH * g + first : PITCH * g + first + cells] for g in range(FIELDS)]

    pad = -3 * FIELDS * cells % TILE
    rows = part(high) + part(low) + part(high) + [jnp.zeros((pad, high.shape[1]), bf16)]
    return jnp.concatenate(rows, axis=0)


def slot(s):
    return 0 if s == 0 else 1 if s == LAYERS - 1 else 2 + s % 3


def kernel(
    lower_hbm_rows,
    upper_hbm_rows,
    phase_hbm,
    jacobian_hbm,
    u_hbm,
    metric_hbm,
    upper_hbm,
    lower_hbm,
    out,
    u,
    metric,
    upper_held,
    lower_held,
    order,
    sorted_own,
    sorted_in,
    partner_ref,
    phase_ref,
    jacobian,
    raw_in,
    basis_own,
    basis_in,
    parts,
    ghost_own,
    ghost_out,
    ghost_in,
    halo_out,
    halo,
    edge_out,
    edge_in,
    edge_add,
    fix,
    pitch_matrix,
    side_matrix,
    pitch_part,
    span_part,
    axial_part,
    small_sem,
    u_sem,
    metric_sem,
    panel_sem,
    send_sem,
    recv_sem,
):
    axial, span = lax.axis_index("axial"), lax.axis_index("span")
    axial_last, span_last = lax.axis_size("axial") - 1, lax.axis_size("span") - 1
    has_left, has_right = axial > 0, axial < axial_last
    has_down, has_up = span > 0, span < span_last
    left = {"axial": jnp.maximum(axial - 1, 0)}
    right = {"axial": jnp.minimum(axial + 1, axial_last)}
    down = {"span": jnp.maximum(span - 1, 0)}
    up = {"span": jnp.minimum(span + 1, span_last)}
    sides = ((has_left, left), (has_right, right))

    barrier = pltpu.get_barrier_semaphore()
    around = sides + ((has_down, down), (has_up, up))
    for present, device in around:

        @pl.when(present)
        def _():
            pl.semaphore_signal(barrier, inc=1, device_id=device, device_id_type=MESH)

    u_copies = [pltpu.make_async_copy(u_hbm.at[:, s], u.at[:, s], u_sem.at[s]) for s in range(LAYERS)]
    metric_copies = [
        pltpu.make_async_copy(metric_hbm.at[:, s], metric.at[:, s], metric_sem.at[s])
        for s in range(LAYERS)
    ]
    panel = (upper_held, lower_held)
    panel_copies = [
        pltpu.make_async_copy(
            hbm.at[:, t * TILE : (t + 1) * TILE], panel[i].at[t], panel_sem.at[i, t]
        )
        for i, hbm in enumerate((upper_hbm, lower_hbm))
        for t in range(TILES)
    ]
    ends, inner = [u_copies[0], u_copies[-1]], u_copies[1:-1]
    small = [
        pltpu.make_async_copy(source, target, small_sem.at[i])
        for i, (source, target) in enumerate(
            (
                (lower_hbm_rows, partner_ref.at[0]),
                (upper_hbm_rows, partner_ref.at[1]),
                (phase_hbm, phase_ref),
                (jacobian_hbm, jacobian),
            )
        )
    ]
    for c in small + panel_copies[:TILES] + ends:
        c.start()

    for i, (present, _) in enumerate(sides):

        @pl.when(jnp.logical_not(present))
        def _():
            sorted_in[i] = jnp.zeros((8, ROWS), f32)
            raw_in[i] = jnp.zeros((2, 8, 128), jnp.int32)
            ghost_in[i] = jnp.zeros((2, FS, ROWS), f32)
            edge_in[i] = jnp.zeros((FIELDS, PITCH, 128), f32)

    for i, present in enumerate((has_down, has_up)):

        @pl.when(jnp.logical_not(present))
        def _():
            halo[i] = jnp.zeros((FIELDS, PITCH, ROWS), bf16)

    for c in small:
        c.wait()
    cosine, sine = jnp.cos(phase_ref[...]), jnp.sin(phase_ref[...])
    upper_sorted = sort_rows(partner_ref[0], cosine, sine, order.at[0])
    lower_sorted = sort_rows(partner_ref[1], cosine, -sine, order.at[1])
    lines = [x for pair in zip(upper_sorted, lower_sorted) for x in pair]
    sorted_own[...] = jnp.concatenate(lines + [jnp.zeros((2, ROWS), f32)], axis=0)

    for c in panel_copies[TILES:]:
        c.start()
    pl.semaphore_wait(barrier, sum(present.astype(jnp.int32) for present, _ in around))

    def remote(number, source, target, device):
        return pltpu.make_async_remote_copy(
            src_ref=source,
            dst_ref=target,
            send_sem=send_sem.at[number],
            recv_sem=recv_sem.at[number],
            device_id=device,
            device_id_type=MESH,
        )

    def tables(i, device):
        return [
            remote(i, sorted_own, sorted_in.at[1 - i], device),
            remote(2 + i, partner_ref, raw_in.at[1 - i], device),
        ]

    def edges(i, device):
        return remote(4 + i, edge_out.at[i], edge_in.at[1 - i], device)

    def ghosts(i, device):
        return remote(6 + i, ghost_out.at[i], ghost_in.at[1 - i], device)

    def halos(i, device):
        return remote(8 + i, halo_out.at[i], halo.at[1 - i], device)

    for i, (present, device) in enumerate(sides):

        @pl.when(present)
        def _():
            for c in tables(i, device):
                c.start()

    for c in ends:
        c.wait()
    halo_out[0] = u[:, 0].astype(bf16)
    halo_out[1] = u[:, LAYERS - 1].astype(bf16)

    for i, (present, device) in enumerate(((has_down, down), (has_up, up))):

        @pl.when(present)
        def _():
            halos(i, device).start()

    fill_stencil(jacobian, (2,), PITCH, pitch_matrix)
    fill_stencil(jacobian, (1, 0), HALF, side_matrix)
    fill_basis(sorted_own[2:4], sorted_own[4:6], basis_own)

    first_row = axial * ROWS

    for i in range(2):
        for c in panel_copies[i * TILES : (i + 1) * TILES]:
            c.wait()
        for c in (inner, metric_copies)[i]:
            c.start()
        evaluate(
            panel[i], basis_own, i, sorted_own[i : i + 1], partner_ref[i], first_row, parts,
            ghost_own.at[i],
        )

    for c in inner:
        c.wait()
    lane = lax.broadcasted_iota(jnp.int32, (PITCH, 128), 1)
    for i, (at, turn) in enumerate(((0, 0), (ROWS - 128, 1))):
        for f in range(FIELDS):
            packed = jnp.zeros((PITCH, 128), f32)
            for s in range(LAYERS):
                turned = u[f, s, :, at : at + 128]
                if (s + turn) % 128:
                    turned = pltpu.roll(turned, s + turn, 1)
                packed = jnp.where(lane == s, turned, packed)
            edge_out[i, f] = packed
    for i, (present, device) in enumerate(sides):

        @pl.when(present)
        def _():
            edges(i, device).start()

    for i, (present, device) in enumerate(sides):

        @pl.when(present)
        def _():
            for c in tables(1 - i, device):
                c.wait_recv()

    odd = axial % 2
    order_in = (odd, 1 - odd)
    fill_basis(
        jnp.concatenate([sorted_in[i, 2:4] for i in order_in], axis=0),
        jnp.concatenate([sorted_in[i, 4:6] for i in order_in], axis=0),
        basis_in,
    )
    for step, i in enumerate(order_in):
        for p in range(2):
            evaluate(
                panel[p], basis_in, 2 * step + p, sorted_in[i, p : p + 1], raw_in[i, p],
                first_row, parts, ghost_out.at[i, p],
            )
        target = axial - 1 + 2 * i

        @pl.when((target >= 0) & (target <= axial_last))
        def _():
            ghosts(i, {"axial": jnp.clip(target, 0, axial_last)}).start()

    def products(s):
        for t in range(TILES):
            at = slice(t * TILE, (t + 1) * TILE)
            high, low = split2(u[:, s, :, at].reshape(FP, TILE))
            x = stacked(high, low, 0, PITCH)
            pitch_part[slot(s), :, at] = jnp.dot(
                pitch_matrix[...], x, preferred_element_type=f32
            )
            for first in (0, HALF):
                x = stacked(high, low, first, HALF)
                y = jnp.dot(side_matrix[...], x, preferred_element_type=f32)
                for f in range(FIELDS):
                    r = slice(PITCH * f + first, PITCH * f + first + HALF)
                    span_part[s + 1, r, at] = y[HALF * f : HALF * (f + 1)]
                    axial_part[slot(s), r, at] = y[HALF * (FIELDS + f) : HALF * (FIELDS + f + 1)]

    def outside(i):
        for t in range(TILES):
            at = slice(t * TILE, (t + 1) * TILE)
            high = halo[i, :, :, at].reshape(FP, TILE)
            for first in (0, HALF):
                x = stacked(high, jnp.zeros_like(high), first, HALF)
                y = jnp.dot(
                    side_matrix[0 : FIELDS * HALF, :], x, preferred_element_type=f32
                )
                for f in range(FIELDS):
                    r = slice(PITCH * f + first, PITCH * f + first + HALF)
                    span_part[i * (LAYERS + 1), r, at] = y[HALF * f : HALF * (f + 1)]

    lane8 = lax.broadcasted_iota(jnp.int32, (8, 128), 1)

    def lower_layer(f, t):
        pair = halo[0, f, 16 * (t // 2) : 16 * (t // 2) + 16, :].astype(f32)
        return pair[8 * (t % 2) : 8 * (t % 2) + 8]

    def combine(s):
        for t in range(PITCH // 8):
            r = slice(8 * t, 8 * t + 8)
            m = [metric[d, s, r, :] for d in range(3)]
            keep = 1.0 - 0.02 * (m[0] + m[1] + m[2])
            for f in range(FIELDS):
                rr = slice(PITCH * f + 8 * t, PITCH * f + 8 * t + 8)
                here = u[f, s, r, :]
                y = axial_part[slot(s), rr, :]
                after = pltpu.roll(y, ROWS - 1, 1)
                before = pltpu.roll(y - 0.02 * here, 1, 1)
                after_in = pltpu.roll(edge_add[1, f, r, :], (127 - s) % 128, 1)
                before_in = edge_add[0, f, r, :]
                if s:
                    before_in = pltpu.roll(before_in, 128 - s, 1)
                along = jnp.concatenate(
                    [
                        after[:, :128] - jnp.where(lane8 == 0, before_in, before[:, :128]),
                        after[:, 128:-128] - before[:, 128:-128],
                        jnp.where(lane8 == 127, after_in, after[:, -128:]) - before[:, -128:],
                    ],
                    axis=1,
                )
                lower = u[f, s - 1, r, :] if s else lower_layer(f, t)
                across = span_part[s + 2, rr, :] - span_part[s, rr, :] + 0.02 * lower
                out[f, s, r, :] = (
                    keep * here + m[2] * pitch_part[slot(s), rr, :] + m[1] * across + m[0] * along
                )

    def patch(s):
        for f in range(FIELDS):
            for i, p in enumerate((0, PITCH - 1)):
                out[f, s, p : p + 1, :] = out[f, s, p : p + 1, :] + fix[i, f, s : s + 1, :]

    for c in metric_copies:
        c.wait()
    products(0)
    products(1)

    for i, (present, device) in enumerate(sides):

        @pl.when(present)
        def _():
            edges(1 - i, device).wait_recv()

    for i, sign in ((0, -0.01), (1, 0.01)):
        for f in range(FIELDS):
            total = sign * edge_in[i, f]
            for g in range(FIELDS):
                total = total + (-0.1 * jacobian[f, 0, g]) * edge_in[i, g]
            edge_add[i, f] = total

    for s in range(2, 6):
        products(s)
        combine(s - 1)

    for i, (present, device) in enumerate(sides):

        @pl.when(present)
        def _():
            ghosts(1 - i, device).wait_recv()

    for i, (present, device) in enumerate(((has_down, down), (has_up, up))):

        @pl.when(present)
        def _():
            halos(1 - i, device).wait_recv()

    for i, (p, sign) in enumerate(((0, 0.1), (PITCH - 1, -0.1))):
        total = ghost_own[i] + ghost_in[0, i] + ghost_in[1, i]
        high, low = split2(total)
        both = jnp.dot(
            jnp.concatenate([high, low], axis=0), order[i], preferred_element_type=f32
        )
        ghost = both[0:FS] + both[FS : 2 * FS]
        scale = jnp.concatenate([metric[2, s, p : p + 1, :] for s in range(LAYERS)], axis=0)
        for f in range(FIELDS):
            total = 0.01 * ghost[f * LAYERS : (f + 1) * LAYERS]
            for g in range(FIELDS):
                total = total + (sign * jacobian[f, 2, g]) * ghost[g * LAYERS : (g + 1) * LAYERS]
            fix[i, f] = scale * total
        outside(i)
        products(6 + i)
        combine(5 + i)
    combine(0)
    combine(LAYERS - 1)
    for s in range(LAYERS):
        patch(s)

    for i, (present, device) in enumerate(sides):

        @pl.when(present)
        def _():
            for c in tables(i, device) + [edges(i, device), ghosts(i, device)]:
                c.wait_send()

    for i, (present, device) in enumerate(((has_down, down), (has_up, up))):

        @pl.when(present)
        def _():
            halos(i, device).wait_send()


def store(held, out, sems):
    copies = [
        pltpu.make_async_copy(held.at[:, s], out.at[:, s], sems.at[s]) for s in range(LAYERS)
    ]
    for c in copies:
        c.start()
    for c in copies:
        c.wait()


def on_device(
    conserved, metric, jacobian, upper_panel, lower_panel, lower_partner, upper_partner, lag_phase
):
    rows = [x.reshape(8, 128) for x in (lower_partner, upper_partner, lag_phase)]
    jacobian = jnp.transpose(jacobian, (1, 0, 2))
    upper = upper_panel.reshape(MODES * FS, ROWS)
    lower = lower_panel.reshape(MODES * FS, ROWS)
    vmem = pl.BlockSpec(memory_space=pltpu.VMEM)
    anywhere = pl.BlockSpec(memory_space=pl.ANY)
    shape = (FIELDS, LAYERS, PITCH, ROWS)
    advanced = pl.pallas_call(
        kernel,
        out_shape=pltpu.VMEM(shape, f32),
        in_specs=[anywhere] * 8,
        out_specs=vmem,
        scratch_shapes=[
            pltpu.VMEM(shape, f32),
            pltpu.VMEM((3, LAYERS, PITCH, ROWS), f32),
            pltpu.VMEM((TILES, MODES * FS, TILE), bf16),
            pltpu.VMEM((TILES, MODES * FS, TILE), bf16),
            pltpu.VMEM((2, ROWS, ROWS), bf16),
            pltpu.VMEM((8, ROWS), f32),
            pltpu.VMEM((2, 8, ROWS), f32),
            pltpu.VMEM((2, 8, 128), jnp.int32),
            pltpu.VMEM((8, 128), f32),
            pltpu.SMEM((FIELDS, 3, FIELDS), f32),
            pltpu.VMEM((2, 2, 8, 128), jnp.int32),
            pltpu.VMEM((TILES, MODES, 8, TILE), f32),
            pltpu.VMEM((TILES, MODES, 8, TILE), f32),
            pltpu.VMEM((PAIRS, FS, TILE), f32),
            pltpu.VMEM((2, FS, ROWS), f32),
            pltpu.VMEM((2, 2, FS, ROWS), f32),
            pltpu.VMEM((2, 2, FS, ROWS), f32),
            pltpu.VMEM((2, FIELDS, PITCH, ROWS), bf16),
            pltpu.VMEM((2, FIELDS, PITCH, ROWS), bf16),
            pltpu.VMEM((2, FIELDS, PITCH, 128), f32),
            pltpu.VMEM((2, FIELDS, PITCH, 128), f32),
            pltpu.VMEM((2, FIELDS, PITCH, 128), f32),
            pltpu.VMEM((2, FIELDS, LAYERS, ROWS), f32),
            pltpu.VMEM((FP, 512), bf16),
            pltpu.VMEM((2 * FIELDS * HALF, TILE), bf16),
            pltpu.VMEM((5, FP, ROWS), f32),
            pltpu.VMEM((LAYERS + 2, FP, ROWS), f32),
            pltpu.VMEM((5, FP, ROWS), f32),
            pltpu.SemaphoreType.DMA((4,)),
            pltpu.SemaphoreType.DMA((LAYERS,)),
            pltpu.SemaphoreType.DMA((LAYERS,)),
            pltpu.SemaphoreType.DMA((2, TILES)),
            pltpu.SemaphoreType.DMA((10,)),
            pltpu.SemaphoreType.DMA((10,)),
        ],
        compiler_params=pltpu.CompilerParams(
            collective_id=0, has_side_effects=True, vmem_limit_bytes=50 * 2**20
        ),
        name="section",
    )(*rows, jacobian, conserved, metric, upper, lower)
    return pl.pallas_call(
        store,
        out_shape=jax.ShapeDtypeStruct(shape, f32),
        in_specs=[vmem],
        out_specs=anywhere,
        scratch_shapes=[pltpu.SemaphoreType.DMA((LAYERS,))],
        compiler_params=pltpu.CompilerParams(vmem_limit_bytes=4 * 2**20),
        name="store",
    )(pltpu.with_memory_space_constraint(advanced, pltpu.VMEM))


def solution(mesh):
    in_specs = (
        P(None, "span", None, "axial"),
        P(None, "span", None, "axial"),
        P(),
        P(None, None, "span", "axial"),
        P(None, None, "span", "axial"),
        P("axial"),
        P("axial"),
        P("axial"),
    )
    out_specs = P(None, "span", None, "axial")
    return jax.shard_map(
        on_device, mesh=mesh, in_specs=in_specs, out_specs=out_specs, check_vma=False
    )
```
